256 devices in a mesh: dp: 256 (over z, x, y, core).
Axes of the slice: x: 4, y: 4, z: 8, core: 2. Of those that a mesh axis runs over, the one named last changes fastest.
Arguments:
- img_feat: bfloat16 [40960, 1152], P('dp'), may hold values from -24 to 24
- txt_feat: bfloat16 [40960, 1152], P('dp'), may hold values from -24 to 24
- img_head: bfloat16 [1152, 1152], replicated, may hold values from -0.1875 to 0.1875
- txt_head: bfloat16 [1152, 1152], replicated, may hold values from -0.1875 to 0.1875
- log_scale: float32 [1], replicated, may hold values from 2 to 3
- logit_bias: float32 [1], replicated, may hold values from -4 to 0
- masks: int32 [2], replicated, may hold values from 1 to 255, as said below
Outputs:
- head_grads: float32 [20736, 128], P('dp')
The draws below stay inside these ranges and needn't reach their ends.
Inputs may be any that keep to these rules, and one draw needn't show every extreme that they name: masks[k] XOR a group's number is its partner group in round k; the 2 masks are distinct.
All inputs are finite; a program needn't handle non-finite values.
Results may differ from the reference program's by a relative error of at most 0.0065.
Values may be sent and summed in bfloat16 or wider, within the bound.
No kernel may reach another device: no remote copies, remote signals or barrier semaphores. Data moves between devices by JAX's collectives and lax.ppermute only.
A program may use at most 128 MiB of HBM per device.

```python
import jax
import jax.numpy as jnp
from jax import lax

D = 1152
ROWS_DEV = 160
ROUNDS = 2
TOKENS = 40960
N_DP = 256


def draw_masks(key, part):
    key = jax.random.fold_in(key, 7)
    first_key, second_key = jax.random.split(key)
    others = jax.random.permutation(first_key, jnp.arange(1, N_DP - 1, dtype=jnp.int32))
    listed = jnp.concatenate([jnp.full((1,), N_DP - 1, dtype=jnp.int32), others[:ROUNDS - 1]])
    placed = jax.random.permutation(second_key, listed)
    return placed.astype(jnp.int32)


def spiked(result, rng, source, target, blocks, factor):
    owner, partner = [(jnp.arange(result.shape[dim]) // (result.shape[dim] // blocks)).reshape([-1 if axis == dim else 1 for axis in range(result.ndim)]) for dim in (source, target)]
    chosen = jax.random.permutation(rng, blocks)[partner]
    strong = (owner == chosen) | (owner == (partner + blocks // 2) % blocks)
    return jnp.where(strong, factor * result, result)


def levels(rng, extent, shards, smallest, top_value):
    gain = 1.0
    for axis_at, shards_of in shards:
        steps = jax.random.uniform(jax.random.fold_in(jax.random.fold_in(rng, 6), axis_at), (shards_of,), jnp.float32, smallest / len(shards), top_value / len(shards))
        gain = gain * jnp.repeat(jnp.exp(steps), extent[axis_at] // shards_of).reshape((-1,) + (1,) * (len(extent) - 1 - axis_at))
    return gain


def centred(key, shape, scale, limit, shards=(), kind=jnp.bfloat16):
    factor_of = levels(key, shape, shards, -0.22, 0.18) if shards else 1.0
    drawn = jax.random.normal(key, shape, jnp.float32) * scale * factor_of
    return jnp.minimum(jnp.maximum(drawn, -limit), limit).astype(kind)


def bell_draw_with(key, shape, scale, limit, cuts, heavy, kind=jnp.bfloat16):
    drawn = scale * jax.random.normal(key, shape, jnp.float32)
    if cuts:
        drawn = drawn * levels(key, shape, cuts, -0.22, 0.18)
    return jnp.clip(spiked(drawn, jax.random.fold_in(key, 3), *heavy), -limit, limit).astype(kind)


def setup_inputs(seed: int = 0) -> dict:
    arg_keys = jax.random.split(jax.random.key(seed), 8)
    return {
        "img_feat": bell_draw_with(arg_keys[0], (TOKENS, D), 1.0, 24.0, ((0, 256),), (0, 1, 128, 5.5)),
        "txt_feat": bell_draw_with(arg_keys[1], (TOKENS, D), 1.0, 24.0, ((0, 256),), (0, 1, 128, 5.5)),
        "img_head": centred(arg_keys[2], (D, D), D ** -0.5, 0.1875),
        "txt_head": centred(arg_keys[3], (D, D), D ** -0.5, 0.1875),
        "log_scale": jnp.clip(jax.random.uniform(arg_keys[4], (1,), jnp.float32, 2.0, 3.0), 2.0, 3.0),
        "logit_bias": jnp.clip(jax.random.uniform(arg_keys[5], (1,), jnp.float32, -4.0, 0.0), -4.0, 0.0),
        "masks": draw_masks(jax.random.fold_in(arg_keys[7], 71), 0),
    }


EPS = 1e-06

def normalize(y):
    r = lax.rsqrt(lax.optimization_barrier(jnp.sum(y * y, axis=-1, keepdims=True)) + EPS)
    return (y * r, r)

def block(za, zc, scale, bias, pos):
    cos = jnp.einsum('nrd,nsd->nrs', za.astype(jnp.float32), zc.astype(jnp.float32))
    logits = scale * cos + bias
    diff = jax.nn.sigmoid(logits) - pos
    grad_b = (diff / 16.0).astype(jnp.bfloat16).astype(jnp.float32)
    dza = scale * jnp.einsum('nrs,nsd->nrd', grad_b, zc.astype(jnp.float32))
    dzc = scale * jnp.einsum('nrs,nrd->nsd', grad_b, za.astype(jnp.float32))
    return (dza, dzc)

def backnorm(dz, z, r):
    return r * (dz - z * lax.optimization_barrier(jnp.sum(z * dz, axis=-1, keepdims=True)))

def reference(img_feat, txt_feat, img_head, txt_head, log_scale, logit_bias, masks):
    yi = jnp.dot(img_feat, img_head, preferred_element_type=jnp.float32)
    yt = jnp.dot(txt_feat, txt_head, preferred_element_type=jnp.float32)
    zi, ri = normalize(yi)
    zt, rt = normalize(yt)
    zib = zi.astype(jnp.bfloat16).reshape(N_DP, ROWS_DEV, D)
    ztb = zt.astype(jnp.bfloat16).reshape(N_DP, ROWS_DEV, D)
    scale = jnp.exp(log_scale[0])
    bias = logit_bias[0]
    eye = jnp.eye(ROWS_DEV, dtype=jnp.float32)[None]
    dzi, dzt = block(zib, ztb, scale, bias, eye)
    groups = jnp.arange(N_DP, dtype=jnp.int32)
    for rnd in range(ROUNDS):
        partner = jnp.bitwise_xor(groups, masks[rnd]).astype(jnp.int32)
        dza, dzc = block(zib, ztb[partner], scale, bias, jnp.zeros_like(eye))
        dzi = dzi + dza
        dzt = dzt + dzc[partner]
    dyi = backnorm(dzi.reshape(TOKENS, D), zi, ri).astype(jnp.bfloat16)
    dyt = backnorm(dzt.reshape(TOKENS, D), zt, rt).astype(jnp.bfloat16)
    dims = (((0,), (0,)), ((), ()))
    grad_img = lax.dot_general(img_feat, dyi, dims, preferred_element_type=jnp.float32)
    grad_txt = lax.dot_general(txt_feat, dyt, dims, preferred_element_type=jnp.float32)
    return jnp.stack([grad_img, grad_txt]).reshape(2 * D * D // 128, 128)
```

```python
import jax
import jax.numpy as jnp
from jax import lax
from jax.experimental import pallas as pl
from jax.experimental.pallas import tpu as pltpu
from jax.sharding import PartitionSpec as P

EPS = 1e-06
AXIS = "dp"
NZ, NX, NY, NCORE = 8, 4, 4, 2
BF = jnp.bfloat16
F32 = jnp.float32
ROWS, WIDTH = 160, 1152
HALF = WIDTH // 2
GROUP = 36
BLOCK = 4 * GROUP
CUTS = ((0, 640), (640, 1152))


def swap(x, flip):
    if flip == 0:
        return x
    return lax.ppermute(x, AXIS, [(i, i ^ flip) for i in range(NZ * NX * NY * NCORE)])


def code(z=0, x=0, y=0, core=0):
    return ((z * NX + x) * NY + y) * NCORE + core


def exchange(feat, masks):
    z = masks // (NX * NY * NCORE)
    xy = masks // NCORE % (NX * NY)
    branches = [
        lambda a, b, p=p, q=q: (swap(a, code(z=p)), swap(b, code(x=q // NY, y=q % NY)))
        for p in range(NZ) for q in range(NX * NY)
    ]

    def leg(at, pair):
        ahead, behind = pair
        ahead, behind = lax.switch(z[at] * 16 + xy[1 - at], branches, ahead, behind)
        return behind, ahead

    return lax.fori_loop(0, 2, leg, (feat, feat))


def dot(a, b, ca=1, cb=0):
    return lax.dot_general(a, b, (((ca,), (cb,)), ((), ())), preferred_element_type=F32)


def normalize(y):
    r = lax.rsqrt(jnp.sum(y * y, axis=-1, keepdims=True) + EPS)
    return y * r, r


def backnorm(dz, z, r):
    return r * (dz - z * jnp.sum(z * dz, axis=-1, keepdims=True))


def row_order():
    me = lax.axis_index(AXIS)
    pos = lax.broadcasted_iota(jnp.int32, (HALF, 1), 0)
    ninth = (pos * 7282) >> 16
    row = pos - 9 * ninth
    z = (ninth & 3) ^ ((me >> 5) & 3)
    x = ((ninth >> 2) & 3) ^ ((me >> 3) & 3)
    y = ((ninth >> 4) & 3) ^ ((me >> 1) & 3)
    src = (((z * 4 + x) * 4 + y) * 2 + (me & 1)) * 9 + row
    feature = lax.broadcasted_iota(jnp.int32, (HALF, WIDTH), 1)
    return jnp.where(feature == src, 1.0, 0.0).astype(BF)


def pick(masks_ref, index, same, other):
    odd = (masks_ref[index] & 1) == 1
    same, other = same[...], other[...]
    return jnp.where(odd, other, same), jnp.where(odd, same, other)


def local_kernel(img_ref, own_ref, same0, same1, other0, other1, ihead_ref, thead_ref,
                 ls_ref, lb_ref, masks_ref, dy_ref):
    first, _ = pick(masks_ref, 0, same0, other0)
    second, _ = pick(masks_ref, 1, same1, other1)
    txt = jnp.concatenate([own_ref[...], first, second], axis=0)
    zi, ri = normalize(dot(img_ref[...], ihead_ref[...]))
    zt, rt = normalize(dot(txt, thead_ref[...]))
    zib = zi.astype(BF)
    ztb = zt.astype(BF)
    scale = jnp.exp(jnp.full((1, 1), ls_ref[0], F32))
    logits = scale * dot(zib, ztb, 1, 1) + lb_ref[0]
    here = lax.broadcasted_iota(jnp.int32, logits.shape, 0) == lax.broadcasted_iota(jnp.int32, logits.shape, 1)
    diff = 1.0 / (1.0 + jnp.exp(-logits)) - jnp.where(here, 1.0, 0.0)
    g = diff / 16.0
    dy_ref[:ROWS, :] = backnorm(scale * dot(g.astype(BF), ztb), zi, ri).astype(BF)
    dy_ref[ROWS:, :] = backnorm(scale * dot(g.T.astype(BF), zib), zt, rt).astype(BF)


def deal_kernel(img_ref, img2_ref, own_ref, own2_ref, same0, same1, other0, other1,
                masks_ref, dimg_ref, dtxt_ref):
    order = row_order()
    first, first2 = pick(masks_ref, 0, same0, other0)
    second, second2 = pick(masks_ref, 1, same1, other1)
    img = jnp.concatenate([img_ref[...], img2_ref[...]], axis=0)
    txt = jnp.concatenate([own_ref[...], first, second, own2_ref[...], first2, second2], axis=0)
    dimg_ref[...] = dot(order, img, 1, 1).astype(BF)
    dtxt_ref[...] = dot(order, txt, 1, 1).astype(BF)


def gradient_kernel(dimg_ref, dtxt_ref, dy_ref, dy2_ref, *outs):
    sides = ((dimg_ref, slice(0, ROWS)), (dtxt_ref, slice(ROWS, 4 * ROWS)))
    for part, (low, high) in enumerate(CUTS):
        wide = high - low
        for side, (dealt_ref, rows) in enumerate(sides):
            dy = jnp.concatenate([dy_ref[rows, low:high], dy2_ref[rows, low:high]], axis=0)
            grad = dot(dealt_ref[...], dy)
            to = slice(side * wide, (side + 1) * wide)
            for d in range(4):
                if part == 0:
                    block = grad[d * BLOCK:(d + 1) * BLOCK]
                else:
                    at = [(y * 4 + d) * GROUP for y in range(4)]
                    block = jnp.concatenate([grad[i:i + GROUP] for i in at], axis=0)
                ref = outs[part * 4 + d]
                ref[:, to] = block.astype(ref.dtype)


def call(kernel, outs, args, scalars, flops):
    bytes_of = lambda xs: sum(x.size * x.dtype.itemsize for x in xs)
    vmem = pl.BlockSpec(memory_space=pltpu.VMEM)
    smem = pl.BlockSpec(memory_space=pltpu.SMEM)
    return pl.pallas_call(
        kernel,
        out_shape=outs,
        in_specs=[vmem] * (len(args) - scalars) + [smem] * scalars,
        out_specs=[vmem] * len(outs),
        compiler_params=pltpu.CompilerParams(vmem_limit_bytes=56 * 2**20),
        cost_estimate=pl.CostEstimate(
            flops=flops, transcendentals=0, bytes_accessed=bytes_of(args) + bytes_of(outs)),
    )(*args)


def shape(rows, cols, kind):
    return jax.ShapeDtypeStruct((rows, cols), kind)


def spread(own, sends, flips):
    got = [[None] * 3, [None] * 3]
    for d in (1, 0, 2):
        for part in (1, 0):
            got[part][d] = swap(sends[part][d], flips[part][d])
    got = lax.optimization_barrier(got)
    return [
        own[part] + got[part][0].astype(F32) + got[part][1].astype(F32) + got[part][2].astype(F32)
        for part in range(2)
    ]


def shards(img_feat, txt_feat, img_head, txt_head, log_scale, logit_bias, masks):
    sibling = code(core=1)
    img2, txt2 = swap(img_feat, sibling), swap(txt_feat, sibling)
    same = exchange(txt_feat, masks)
    img2, txt2, same = lax.optimization_barrier((img2, txt2, same))
    others = [swap(x, sibling) for x in same]
    dy, = call(
        local_kernel, [shape(4 * ROWS, WIDTH, BF)],
        [img_feat, txt_feat, *same, *others, img_head, txt_head, log_scale, logit_bias, masks],
        3, 3 * 10**9)
    dy2 = swap(dy, sibling)
    dealt = call(
        deal_kernel, [shape(HALF, 2 * ROWS, BF), shape(HALF, 6 * ROWS, BF)],
        [img_feat, img2, txt_feat, txt2, *same, *others, masks], 1, 2 * 10**9)
    blocks = call(
        gradient_kernel,
        [shape(BLOCK, 2 * (high - low), F32 if d == 0 else BF) for low, high in CUTS for d in range(4)],
        [*dealt, dy, dy2], 0, 2 * 10**9)

    along_y = [code(y=d) for d in (1, 2, 3)]
    along_x = [code(x=d) for d in (1, 2, 3)]
    sums = spread(
        (blocks[0], blocks[4]), (blocks[1:4], blocks[5:8]), (along_y, along_x))
    rows = [slice(d * GROUP, (d + 1) * GROUP) for d in range(4)]
    sums = spread(
        [s[rows[0]] for s in sums],
        [[s[rows[d]].astype(BF) for d in (1, 2, 3)] for s in sums],
        (along_x, along_y))

    img, txt = (
        jnp.concatenate([s[:, side * (s.shape[1] // 2):(side + 1) * (s.shape[1] // 2)] for s in sums], axis=1)
        for side in range(2)
    )
    high = lax.axis_index(AXIS) >= code(z=4)
    near, far = jnp.where(high, txt, img), jnp.where(high, img, txt)
    total = near[:9]
    for d in range(1, 8):
        rows = (far if d >= 4 else near)[(d & 3) * 9:(d & 3) * 9 + 9]
        total = total + swap(rows.astype(BF), code(z=d)).astype(F32)
    return total.reshape(81, 128)


def solution(mesh):
    return jax.shard_map(
        shards,
        mesh=mesh,
        in_specs=(P("dp", None), P("dp", None), P(), P(), P(), P(), P()),
        out_specs=P("dp", None),
        check_vma=False,
    )
```

```python
import jax
import jax.numpy as jnp
from jax import lax
from jax.experimental import pallas as pl
from jax.experimental.pallas import tpu as pltpu
from jax.sharding import PartitionSpec as P

EPS = 1e-06
AXIS = "dp"
NZ, NX, NY, NCORE = 8, 4, 4, 2
BF = jnp.bfloat16
F32 = jnp.float32
ROWS, WIDTH = 160, 1152
HALF = WIDTH // 2
GROUP = 36
BLOCK = 4 * GROUP
CUTS = ((0, 640), (640, 1152))


def swap(x, flip):
    if flip == 0:
        return x
    return lax.ppermute(x, AXIS, [(i, i ^ flip) for i in range(NZ * NX * NY * NCORE)])


def code(z=0, x=0, y=0, core=0):
    return ((z * NX + x) * NY + y) * NCORE + core


def exchange(feat, other, masks):
    core = lax.axis_index(AXIS) % NCORE
    mine = masks[core]
    along_z = mine // (NX * NY * NCORE)
    along_xy = NZ + mine // NCORE % (NX * NY)
    flips = [code(z=p) for p in range(NZ)] + [code(x=q // NY, y=q % NY) for q in range(NX * NY)]
    branches = [lambda a, flip=flip: swap(a, flip) for flip in flips]
    near = jnp.where(core == 0, feat, other)
    far = jnp.where(core == 0, other, feat)
    got = jnp.concatenate([near, far], axis=0)
    got = lax.switch(jnp.where(core == 0, along_z, along_xy), branches, got)
    return lax.switch(jnp.where(core == 0, along_xy, along_z), branches, got)


def dot(a, b, ca=1, cb=0):
    return lax.dot_general(a, b, (((ca,), (cb,)), ((), ())), preferred_element_type=F32)


def normalize(y):
    r = lax.rsqrt(jnp.sum(y * y, axis=-1, keepdims=True) + EPS)
    return y * r, r


def backnorm(dz, z, r):
    return r * (dz - z * jnp.sum(z * dz, axis=-1, keepdims=True))


def row_order():
    me = lax.axis_index(AXIS)
    pos = lax.broadcasted_iota(jnp.int32, (HALF, 1), 0)
    ninth = (pos * 7282) >> 16
    row = pos - 9 * ninth
    z = (ninth & 3) ^ ((me >> 5) & 3)
    x = ((ninth >> 2) & 3) ^ ((me >> 3) & 3)
    y = ((ninth >> 4) & 3) ^ ((me >> 1) & 3)
    src = (((z * 4 + x) * 4 + y) * 2 + (me & 1)) * 9 + row
    feature = lax.broadcasted_iota(jnp.int32, (HALF, WIDTH), 1)
    return jnp.where(feature == src, 1.0, 0.0).astype(BF)


def partners(masks_ref, mine_ref, theirs_ref, dcore):
    core = lax.axis_index(AXIS) & 1
    found = []
    for ref, index in ((mine_ref, core), (theirs_ref, 1 - core)):
        at = (core ^ dcore) ^ (masks_ref[index] & 1)
        found.append(ref[pl.ds(pl.multiple_of(at * ROWS, ROWS), ROWS), :])
    return found


def local_kernel(img_ref, own_ref, mine_ref, theirs_ref, ihead_ref, thead_ref,
                 ls_ref, lb_ref, masks_ref, dy_ref):
    txt = jnp.concatenate([own_ref[...], *partners(masks_ref, mine_ref, theirs_ref, 0)], axis=0)
    zi, ri = normalize(dot(img_ref[...], ihead_ref[...]))
    zt, rt = normalize(dot(txt, thead_ref[...]))
    zib = zi.astype(BF)
    ztb = zt.astype(BF)
    scale = jnp.exp(jnp.full((1, 1), ls_ref[0], F32))
    logits = scale * dot(zib, ztb, 1, 1) + lb_ref[0]
    here = lax.broadcasted_iota(jnp.int32, logits.shape, 0) == lax.broadcasted_iota(jnp.int32, logits.shape, 1)
    diff = 1.0 / (1.0 + jnp.exp(-logits)) - jnp.where(here, 1.0, 0.0)
    g = diff / 16.0
    dy_ref[:ROWS, :] = backnorm(scale * dot(g.astype(BF), ztb), zi, ri).astype(BF)
    dy_ref[ROWS:, :] = backnorm(scale * dot(g.T.astype(BF), zib), zt, rt).astype(BF)


def deal_kernel(img_ref, img2_ref, own_ref, own2_ref, mine_ref, theirs_ref,
                masks_ref, dimg_ref, dtxt_ref):
    order = row_order()
    ours = partners(masks_ref, mine_ref, theirs_ref, 0)
    others = partners(masks_ref, mine_ref, theirs_ref, 1)
    img = jnp.concatenate([img_ref[...], img2_ref[...]], axis=0)
    txt = jnp.concatenate([own_ref[...], *ours, own2_ref[...], *others[::-1]], axis=0)
    dimg_ref[...] = dot(order, img, 1, 1).astype(BF)
    dtxt_ref[...] = dot(order, txt, 1, 1).astype(BF)


def gradient_kernel(dimg_ref, dtxt_ref, dy_ref, dy2_ref, *outs):
    sides = ((dimg_ref, slice(0, ROWS)), (dtxt_ref, slice(ROWS, 4 * ROWS)))
    for part, (low, high) in enumerate(CUTS):
        wide = high - low
        for side, (dealt_ref, rows) in enumerate(sides):
            dy = jnp.concatenate([dy_ref[rows, low:high], dy2_ref[rows, low:high]], axis=0)
            grad = dot(dealt_ref[...], dy)
            to = slice(side * wide, (side + 1) * wide)
            for d in range(4):
                if part == 0:
                    block = grad[d * BLOCK:(d + 1) * BLOCK]
                else:
                    at = [(y * 4 + d) * GROUP for y in range(4)]
                    block = jnp.concatenate([grad[i:i + GROUP] for i in at], axis=0)
                ref = outs[part * 4 + d]
                ref[:, to] = block.astype(ref.dtype)


def call(kernel, outs, args, scalars, flops):
    bytes_of = lambda xs: sum(x.size * x.dtype.itemsize for x in xs)
    vmem = pl.BlockSpec(memory_space=pltpu.VMEM)
    smem = pl.BlockSpec(memory_space=pltpu.SMEM)
    return pl.pallas_call(
        kernel,
        out_shape=outs,
        in_specs=[vmem] * (len(args) - scalars) + [smem] * scalars,
        out_specs=[vmem] * len(outs),
        compiler_params=pltpu.CompilerParams(vmem_limit_bytes=28 * 2**20),
        cost_estimate=pl.CostEstimate(
            flops=flops, transcendentals=0, bytes_accessed=bytes_of(args) + bytes_of(outs)),
    )(*args)


def shape(rows, cols, kind):
    return jax.ShapeDtypeStruct((rows, cols), kind)


def spread(own, sends, flips):
    got = [[None] * 3, [None] * 3]
    for d in (1, 0, 2):
        for part in (1, 0):
            got[part][d] = swap(sends[part][d], flips[part][d])
    got = lax.optimization_barrier(got)
    return [
        own[part] + got[part][0].astype(F32) + got[part][1].astype(F32) + got[part][2].astype(F32)
        for part in range(2)
    ]


def shards(img_feat, txt_feat, img_head, txt_head, log_scale, logit_bias, masks):
    sibling = code(core=1)
    img2, txt2 = swap(img_feat, sibling), swap(txt_feat, sibling)
    mine = exchange(txt_feat, txt2, masks)
    img2, mine = lax.optimization_barrier((img2, mine))
    theirs = swap(mine, sibling)
    dy, = call(
        local_kernel, [shape(4 * ROWS, WIDTH, BF)],
        [img_feat, txt_feat, mine, theirs, img_head, txt_head, log_scale, logit_bias, masks],
        3, 3 * 10**9)
    dy2 = swap(dy, sibling)
    dealt = call(
        deal_kernel, [shape(HALF, 2 * ROWS, BF), shape(HALF, 6 * ROWS, BF)],
        [img_feat, img2, txt_feat, txt2, mine, theirs, masks], 1, 2 * 10**9)
    blocks = call(
        gradient_kernel,
        [shape(BLOCK, 2 * (high - low), F32 if d == 0 else BF) for low, high in CUTS for d in range(4)],
        [*dealt, dy, dy2], 0, 2 * 10**9)

    along_y = [code(y=d) for d in (1, 2, 3)]
    along_x = [code(x=d) for d in (1, 2, 3)]
    sums = spread(
        (blocks[0], blocks[4]), (blocks[1:4], blocks[5:8]), (along_y, along_x))
    rows = [slice(d * GROUP, (d + 1) * GROUP) for d in range(4)]
    sums = spread(
        [s[rows[0]] for s in sums],
        [[s[rows[d]].astype(BF) for d in (1, 2, 3)] for s in sums],
        (along_x, along_y))

    img, txt = (
        jnp.concatenate([s[:, side * (s.shape[1] // 2):(side + 1) * (s.shape[1] // 2)] for s in sums], axis=1)
        for side in range(2)
    )
    high = lax.axis_index(AXIS) >= code(z=4)
    near, far = jnp.where(high, txt, img), jnp.where(high, img, txt)
    total = near[:9]
    for d in range(1, 8):
        rows = (far if d >= 4 else near)[(d & 3) * 9:(d & 3) * 9 + 9]
        total = total + swap(rows.astype(BF), code(z=d)).astype(F32)
    return total.reshape(81, 128)


def solution(mesh):
    return jax.shard_map(
        shards,
        mesh=mesh,
        in_specs=(P("dp", None), P("dp", None), P(), P(), P(), P(), P()),
        out_specs=P("dp", None),
        check_vma=False,
    )
```

```python
import jax
import jax.numpy as jnp
from jax import lax
from jax.experimental import pallas as pl
from jax.experimental.pallas import tpu as pltpu
from jax.sharding import PartitionSpec as P

EPS = 1e-06
AXIS = "dp"
NZ, NX, NY, NCORE = 8, 4, 4, 2
BF = jnp.bfloat16
F32 = jnp.float32
ROWS, WIDTH = 160, 1152
HALF = WIDTH // 2
GROUP = 36
BLOCK = 4 * GROUP


def swap(x, flip, odd_flip=None):
    if flip == 0:
        return x
    flips = (flip, flip if odd_flip is None else odd_flip)
    return lax.ppermute(x, AXIS, [(i, i ^ flips[i % NCORE]) for i in range(NZ * NX * NY * NCORE)])


def code(z=0, x=0, y=0, core=0):
    return ((z * NX + x) * NY + y) * NCORE + core


def exchange(feat, other, masks):
    core = lax.axis_index(AXIS) % NCORE
    mine = jnp.where(core == 0, masks[0], masks[1])
    along_z = mine // (NX * NY * NCORE)
    along_xy = NZ + mine // NCORE % (NX * NY)
    flips = [code(z=p) for p in range(NZ)] + [code(x=q // NY, y=q % NY) for q in range(NX * NY)]
    branches = [lambda a, flip=flip: swap(a, flip) for flip in flips]
    got = jnp.concatenate([feat, other], axis=0)
    got = lax.switch(jnp.where(core == 0, along_z, along_xy), branches, got)
    return lax.switch(jnp.where(core == 0, along_xy, along_z), branches, got)


def dot(a, b, ca=1, cb=0):
    return lax.dot_general(a, b, (((ca,), (cb,)), ((), ())), preferred_element_type=F32)


def normalize(y):
    r = lax.rsqrt(jnp.sum(y * y, axis=-1, keepdims=True) + EPS)
    return y * r, r


def backnorm(dz, z, r):
    return r * (dz - z * jnp.sum(z * dz, axis=-1, keepdims=True))


def row_order():
    me = lax.axis_index(AXIS)
    core = me & 1
    pos = lax.broadcasted_iota(jnp.int32, (HALF, 1), 0)
    ninth = (pos * 7282) >> 16
    row = pos - 9 * ninth
    inner, outer = (ninth >> 2) & 3, (ninth >> 4) & 3
    z = (ninth & 3) ^ ((me >> 5) & 3)
    x = jnp.where(core == 0, inner, outer) ^ ((me >> 3) & 3)
    y = jnp.where(core == 0, outer, inner) ^ ((me >> 1) & 3)
    src = (((z * 4 + x) * 4 + y) * 2 + core) * 9 + row
    feature = lax.broadcasted_iota(jnp.int32, (HALF, WIDTH), 1)
    return jnp.where(feature == src, 1.0, 0.0).astype(BF)


def partners(masks_ref, mine_ref, theirs_ref, dcore):
    core = lax.axis_index(AXIS) & 1
    found = []
    for ref, index, fetcher in ((mine_ref, core, 0), (theirs_ref, 1 - core, 1)):
        at = (masks_ref[index] & 1) ^ (dcore ^ fetcher)
        found.append(ref[pl.ds(pl.multiple_of(at * ROWS, ROWS), ROWS), :])
    return found


def own_kernel(img_ref, img2_ref, txt_ref, txt2_ref, ihead_ref, yi_ref, dimg_ref, dtxt_ref):
    yi_ref[...] = dot(img_ref[...], ihead_ref[...])
    order = row_order()
    dimg_ref[...] = dot(order, jnp.concatenate([img_ref[...], img2_ref[...]], axis=0), 1, 1).astype(BF)
    dtxt_ref[...] = dot(order, jnp.concatenate([txt_ref[...], txt2_ref[...]], axis=0), 1, 1).astype(BF)


def local_kernel(yi_ref, txt_ref, mine_ref, theirs_ref, thead_ref, ls_ref, lb_ref, masks_ref, dy_ref):
    txt = jnp.concatenate([txt_ref[...], *partners(masks_ref, mine_ref, theirs_ref, 0)], axis=0)
    zi, ri = normalize(yi_ref[...])
    zt, rt = normalize(dot(txt, thead_ref[...]))
    zib = zi.astype(BF)
    ztb = zt.astype(BF)
    scale = jnp.exp(jnp.full((1, 1), ls_ref[0], F32))
    logits = scale * dot(zib, ztb, 1, 1) + lb_ref[0]
    here = lax.broadcasted_iota(jnp.int32, logits.shape, 0) == lax.broadcasted_iota(jnp.int32, logits.shape, 1)
    diff = 1.0 / (1.0 + jnp.exp(-logits)) - jnp.where(here, 1.0, 0.0)
    g = diff / 16.0
    dy_ref[:ROWS, :] = backnorm(scale * dot(g.astype(BF), ztb), zi, ri).astype(BF)
    dy_ref[ROWS:, :] = backnorm(scale * dot(g.T.astype(BF), zib), zt, rt).astype(BF)


def deal_kernel(mine_ref, theirs_ref, masks_ref, dtxt_ref):
    ours = partners(masks_ref, mine_ref, theirs_ref, 0)
    others = partners(masks_ref, mine_ref, theirs_ref, 1)
    found = jnp.concatenate([*ours, *others[::-1]], axis=0)
    dtxt_ref[...] = dot(row_order(), found, 1, 1).astype(BF)


def gradient_kernel(dimg_ref, dtxt_ref, dfound_ref, dy_ref, dy2_ref, *outs):
    def both(low, high):
        return jnp.concatenate([dy_ref[low:high, :], dy2_ref[low:high, :]], axis=0)

    img = dot(dimg_ref[...], both(0, ROWS))
    txt = dot(dtxt_ref[...], both(ROWS, 2 * ROWS)) + dot(dfound_ref[...], both(2 * ROWS, 4 * ROWS))
    for d, ref in enumerate(outs):
        ref[:, :WIDTH] = img[d * BLOCK:(d + 1) * BLOCK].astype(ref.dtype)
        ref[:, WIDTH:] = txt[d * BLOCK:(d + 1) * BLOCK].astype(ref.dtype)


def call(kernel, outs, args, scalars, flops):
    bytes_of = lambda xs: sum(x.size * x.dtype.itemsize for x in xs)
    vmem = pl.BlockSpec(memory_space=pltpu.VMEM)
    smem = pl.BlockSpec(memory_space=pltpu.SMEM)
    return pl.pallas_call(
        kernel,
        out_shape=outs,
        in_specs=[vmem] * (len(args) - scalars) + [smem] * scalars,
        out_specs=[vmem] * len(outs),
        compiler_params=pltpu.CompilerParams(vmem_limit_bytes=28 * 2**20),
        cost_estimate=pl.CostEstimate(
            flops=flops, transcendentals=0, bytes_accessed=bytes_of(args) + bytes_of(outs)),
    )(*args)


def shape(rows, cols, kind):
    return jax.ShapeDtypeStruct((rows, cols), kind)


def spread(own, sends, flips):
    got = [None] * len(sends)
    for i in (1, 0, 2):
        got[i] = swap(sends[i], *flips[i])
    got = lax.optimization_barrier(got)
    return own + got[0].astype(F32) + got[1].astype(F32) + got[2].astype(F32)


def shards(img_feat, txt_feat, img_head, txt_head, log_scale, logit_bias, masks):
    sibling = code(core=1)
    img2, txt2 = swap(img_feat, sibling), swap(txt_feat, sibling)
    mine = exchange(txt_feat, txt2, masks)
    img, txt, img2, txt2, mine = lax.optimization_barrier((img_feat, txt_feat, img2, txt2, mine))
    theirs = swap(mine, sibling)
    yi, dimg, dtxt = call(
        own_kernel,
        [shape(ROWS, WIDTH, F32)] + [shape(HALF, 2 * ROWS, BF)] * 2,
        [img, img2, txt, txt2, img_head], 0, 2 * 10**9)
    dy, = call(
        local_kernel, [shape(4 * ROWS, WIDTH, BF)],
        [yi, txt, mine, theirs, txt_head, log_scale, logit_bias, masks], 3, 2 * 10**9)
    dy2 = swap(dy, sibling)
    dfound, = call(deal_kernel, [shape(HALF, 4 * ROWS, BF)], [mine, theirs, masks], 1, 10**9)
    own, *sends = call(
        gradient_kernel,
        [shape(BLOCK, 2 * WIDTH, F32 if d == 0 else BF) for d in range(4)],
        [dimg, dtxt, dfound, dy, dy2], 0, 2 * 10**9)

    total = spread(own, sends, [(code(y=d), code(x=d)) for d in (1, 2, 3)])
    rows = [total[d * GROUP:(d + 1) * GROUP] for d in range(4)]
    total = spread(rows[0], [r.astype(BF) for r in rows[1:]], [(code(x=d), code(y=d)) for d in (1, 2, 3)])

    high = lax.axis_index(AXIS) >= code(z=4)
    img, txt = total[:, :WIDTH], total[:, WIDTH:]
    near, far = jnp.where(high, txt, img), jnp.where(high, img, txt)
    far = jnp.concatenate([far[i * 9:i * 9 + 9] for i in (3, 2, 1, 0)], axis=0)
    total = near + swap(far.astype(BF), code(z=7)).astype(F32)
    rows = [total[d * 9:d * 9 + 9] for d in range(4)]
    total = spread(rows[0], [r.astype(BF) for r in rows[1:]], [(code(z=d),) for d in (1, 2, 3)])
    return total.reshape(81, 128)


def solution(mesh):
    return jax.shard_map(
        shards,
        mesh=mesh,
        in_specs=(P("dp", None), P("dp", None), P(), P(), P(), P(), P()),
        out_specs=P("dp", None),
        check_vma=False,
    )
```

```python
import functools

import jax
import jax.numpy as jnp
from jax import lax
from jax.experimental import pallas as pl
from jax.experimental.pallas import tpu as pltpu
from jax.sharding import PartitionSpec as P

EPS = 1e-06
AXIS = "dp"
NZ, NX, NY, NCORE = 8, 4, 4, 2
BF = jnp.bfloat16
F32 = jnp.float32
ROWS, WIDTH = 160, 1152
HALF = WIDTH // 2
GROUP = 36
BLOCK = 4 * GROUP


def swap(x, flip, odd_flip=None):
    flips = (flip, flip if odd_flip is None else odd_flip)
    return lax.ppermute(x, AXIS, [(i, i ^ flips[i % NCORE]) for i in range(NZ * NX * NY * NCORE)])


def code(z=0, x=0, y=0, core=0):
    return ((z * NX + x) * NY + y) * NCORE + core


def exchange(feat, other, masks):
    core = lax.axis_index(AXIS) % NCORE
    mine = jnp.where(core == 0, masks[0], masks[1])
    along_z = mine // (NX * NY * NCORE)
    along_xy = NZ + mine // NCORE % (NX * NY)
    flips = [code(z=p) for p in range(NZ)] + [code(x=q // NY, y=q % NY) for q in range(NX * NY)]
    branches = [lambda a, f=f: swap(a, f) if f else a for f in flips]
    got = jnp.concatenate([feat, other], axis=0)
    got = lax.switch(jnp.where(core == 0, along_z, along_xy), branches, got)
    return lax.switch(jnp.where(core == 0, along_xy, along_z), branches, got)


def dot(a, b, ca=1, cb=0):
    return lax.dot_general(a, b, (((ca,), (cb,)), ((), ())), preferred_element_type=F32)


def normalize(y):
    r = lax.rsqrt(jnp.sum(y * y, axis=-1, keepdims=True) + EPS)
    return y * r, r


def backnorm(dz, z, r):
    return r * (dz - z * jnp.sum(z * dz, axis=-1, keepdims=True))


def row_order():
    me = lax.axis_index(AXIS)
    core = me & 1
    pos = lax.broadcasted_iota(jnp.int32, (HALF, 1), 0)
    ninth = (pos * 7282) >> 16
    row = pos - 9 * ninth
    inner, outer = (ninth >> 2) & 3, (ninth >> 4) & 3
    z = (ninth & 3) ^ ((me >> 5) & 3)
    x = jnp.where(core == 0, inner, outer) ^ ((me >> 3) & 3)
    y = jnp.where(core == 0, outer, inner) ^ ((me >> 1) & 3)
    src = (((z * 4 + x) * 4 + y) * 2 + core) * 9 + row
    feature = lax.broadcasted_iota(jnp.int32, (HALF, WIDTH), 1)
    return jnp.where(feature == src, 1.0, 0.0).astype(BF)


def partners(masks_ref, mine_ref, theirs_ref, dcore):
    core = lax.axis_index(AXIS) & 1
    found = []
    for ref, index, fetcher in ((mine_ref, core, 0), (theirs_ref, 1 - core, 1)):
        at = (masks_ref[index] & 1) ^ (dcore ^ fetcher)
        found.append(ref[pl.ds(pl.multiple_of(at * ROWS, ROWS), ROWS), :])
    return found


def own_kernel(img_ref, txt_ref, ihead_ref, yi_ref, dimg_ref, dtxt_ref):
    yi_ref[...] = dot(img_ref[...], ihead_ref[...])
    order = row_order()
    dimg_ref[...] = dot(order, img_ref[...], 1, 1).astype(BF)
    dtxt_ref[...] = dot(order, txt_ref[...], 1, 1).astype(BF)


def local_kernel(yi_ref, txt_ref, mine_ref, theirs_ref, thead_ref, ls_ref, lb_ref, masks_ref, dy_ref):
    txt = jnp.concatenate([txt_ref[...], *partners(masks_ref, mine_ref, theirs_ref, 0)], axis=0)
    zi, ri = normalize(yi_ref[...])
    zt, rt = normalize(dot(txt, thead_ref[...]))
    zib = zi.astype(BF)
    ztb = zt.astype(BF)
    scale = jnp.exp(jnp.full((1, 1), ls_ref[0], F32))
    logits = scale * dot(zib, ztb, 1, 1) + lb_ref[0]
    here = lax.broadcasted_iota(jnp.int32, logits.shape, 0) == lax.broadcasted_iota(jnp.int32, logits.shape, 1)
    diff = 1.0 / (1.0 + jnp.exp(-logits)) - jnp.where(here, 1.0, 0.0)
    g = diff / 16.0
    dy_ref[:ROWS, :] = backnorm(scale * dot(g.astype(BF), ztb), zi, ri).astype(BF)
    dy_ref[ROWS:, :] = backnorm(scale * dot(g.T.astype(BF), zib), zt, rt).astype(BF)


def deal_kernel(img2_ref, txt2_ref, mine_ref, theirs_ref, masks_ref, dimg_ref, dtxt_ref):
    order = row_order()
    ours = partners(masks_ref, mine_ref, theirs_ref, 0)
    others = partners(masks_ref, mine_ref, theirs_ref, 1)
    dimg_ref[...] = dot(order, img2_ref[...], 1, 1).astype(BF)
    txt = jnp.concatenate([txt2_ref[...], *ours, *others[::-1]], axis=0)
    dtxt_ref[...] = dot(order, txt, 1, 1).astype(BF)


def gradient_kernel(distances, dimg_ref, dtxt_ref, dimg2_ref, dtxt2_ref, dy_ref, dy2_ref, *outs):
    dy2_txt = jnp.concatenate(
        [dy2_ref[ROWS:2 * ROWS, :], dy_ref[2 * ROWS:, :], dy2_ref[2 * ROWS:, :]], axis=0)
    for d, ref in zip(distances, outs):
        rows = slice(d * BLOCK, (d + 1) * BLOCK)
        img = dot(dimg_ref[rows, :], dy_ref[:ROWS, :]) + dot(dimg2_ref[rows, :], dy2_ref[:ROWS, :])
        txt = dot(dtxt_ref[rows, :], dy_ref[ROWS:2 * ROWS, :]) + dot(dtxt2_ref[rows, :], dy2_txt)
        ref[:, :WIDTH] = img.astype(ref.dtype)
        ref[:, WIDTH:] = txt.astype(ref.dtype)


def call(kernel, outs, args, scalars, flops):
    bytes_of = lambda xs: sum(x.size * x.dtype.itemsize for x in xs)
    vmem = pl.BlockSpec(memory_space=pltpu.VMEM)
    smem = pl.BlockSpec(memory_space=pltpu.SMEM)
    return pl.pallas_call(
        kernel,
        out_shape=outs,
        in_specs=[vmem] * (len(args) - scalars) + [smem] * scalars,
        out_specs=[vmem] * len(outs),
        compiler_params=pltpu.CompilerParams(vmem_limit_bytes=28 * 2**20),
        cost_estimate=pl.CostEstimate(
            flops=flops, transcendentals=0, bytes_accessed=bytes_of(args) + bytes_of(outs)),
    )(*args)


def shape(rows, cols, kind):
    return jax.ShapeDtypeStruct((rows, cols), kind)


def spread(own, sends, flips):
    got = [None] * len(sends)
    for i in (1, 0, 2):
        got[i] = swap(sends[i], *flips[i])
    got = lax.optimization_barrier(got)
    return own + got[0].astype(F32) + got[1].astype(F32) + got[2].astype(F32)


def shards(img_feat, txt_feat, img_head, txt_head, log_scale, logit_bias, masks):
    sibling = code(core=1)
    img2, txt2 = swap(img_feat, sibling), swap(txt_feat, sibling)
    mine = exchange(txt_feat, txt2, masks)
    img, txt, img2, txt2, mine = lax.optimization_barrier((img_feat, txt_feat, img2, txt2, mine))
    theirs = swap(mine, sibling)
    yi, dimg, dtxt = call(
        own_kernel, [shape(ROWS, WIDTH, F32)] + [shape(HALF, ROWS, BF)] * 2, [img, txt, img_head], 0, 10**9)
    dy, = call(
        local_kernel, [shape(4 * ROWS, WIDTH, BF)],
        [yi, txt, mine, theirs, txt_head, log_scale, logit_bias, masks], 3, 2 * 10**9)
    dy2 = swap(dy, sibling)
    dimg2, dtxt2 = call(
        deal_kernel, [shape(HALF, ROWS, BF), shape(HALF, 5 * ROWS, BF)],
        [img2, txt2, mine, theirs, masks], 1, 2 * 10**9)

    def blocks(distances, kind):
        return call(
            functools.partial(gradient_kernel, distances), [shape(BLOCK, 2 * WIDTH, kind)] * len(distances),
            [dimg, dtxt, dimg2, dtxt2, dy, dy2], 0, len(distances) * 4 * 10**8)

    second, = blocks((2,), BF)
    first, third = blocks((1, 3), BF)
    kept, = blocks((0,), F32)
    total = spread(kept, (first, second, third), [(code(y=d), code(x=d)) for d in (1, 2, 3)])
    rows = [total[d * GROUP:(d + 1) * GROUP] for d in range(4)]
    total = spread(rows[0], [r.astype(BF) for r in rows[1:]], [(code(x=d), code(y=d)) for d in (1, 2, 3)])

    high = lax.axis_index(AXIS) >= code(z=4)
    img, txt = total[:, :WIDTH], total[:, WIDTH:]
    near, far = jnp.where(high, txt, img), jnp.where(high, img, txt)
    far = jnp.concatenate([far[i * 9:i * 9 + 9] for i in (3, 2, 1, 0)], axis=0)
    total = near + swap(far.astype(BF), code(z=7)).astype(F32)
    rows = [total[d * 9:d * 9 + 9] for d in range(4)]
    total = spread(rows[0], [r.astype(BF) for r in rows[1:]], [(code(z=d),) for d in (1, 2, 3)])
    return total.reshape(81, 128)


def solution(mesh):
    return jax.shard_map(
        shards,
        mesh=mesh,
        in_specs=(P("dp", None), P("dp", None), P(), P(), P(), P(), P()),
        out_specs=P("dp", None),
        check_vma=False,
    )
```

```python
import functools

import jax
import jax.numpy as jnp
from jax import lax
from jax.experimental import pallas as pl
from jax.experimental.pallas import tpu as pltpu
from jax.sharding import PartitionSpec as P

EPS = 1e-06
AXIS = "dp"
NZ, NX, NY, NCORE = 8, 4, 4, 2
BF = jnp.bfloat16
F32 = jnp.float32
ROWS, WIDTH = 160, 1152
HALF = WIDTH // 2
GROUP = 36
BLOCK = 4 * GROUP


def swap(x, flip, odd_flip=None):
    flips = (flip, flip if odd_flip is None else odd_flip)
    return lax.ppermute(x, AXIS, [(i, i ^ flips[i % NCORE]) for i in range(NZ * NX * NY * NCORE)])


def code(z=0, x=0, y=0, core=0):
    return ((z * NX + x) * NY + y) * NCORE + core


def plan(first, second):
    both = first ^ second
    low, high = jnp.minimum(first, second), jnp.maximum(first, second)
    return jnp.maximum(high, both), jnp.minimum(low, both), both


def start_kernel(img_hbm, txt_hbm, masks_ref, own_ref, first_ref, second_ref, arrived):
    even = lax.axis_index(AXIS) & 1 == 0

    @pl.when(even)
    def _():
        pltpu.make_async_copy(txt_hbm, own_ref, arrived).start()

    @pl.when(jnp.logical_not(even))
    def _():
        pltpu.make_async_copy(img_hbm, own_ref, arrived).start()

    by_text, by_image, _ = plan(masks_ref[0], masks_ref[1])
    mask = jnp.where(even, by_text, by_image)
    along_z = mask >> 5
    along_xy = NZ + ((mask >> 1) & 15)
    first_ref[0] = jnp.where(even, along_z, along_xy)
    second_ref[0] = jnp.where(even, along_xy, along_z)
    pltpu.make_async_copy(txt_hbm, own_ref, arrived).wait()


def exchange(img, txt, img2, txt2, masks):
    even = lax.axis_index(AXIS) & 1 == 0
    flips = [code(z=p) for p in range(NZ)] + [code(x=q // NY, y=q % NY) for q in range(NX * NY)]
    branches = [lambda a, f=f: swap(a, f) if f else a for f in flips]
    index = jax.ShapeDtypeStruct((1,), jnp.int32)
    own, first, second = call(
        start_kernel, [shape(ROWS, WIDTH, BF), index, index], [img, txt, masks], 1, 10**6, scalar_outs=2,
        grant=60, placed=pl.ANY, scratch=[pltpu.SemaphoreType.DMA])
    got = jnp.concatenate([own, jnp.where(even, txt2, img2)], axis=0)
    got = lax.switch(first[0], branches, got)
    return lax.switch(second[0], branches, got)


def dot(a, b, ca=1, cb=0):
    return lax.dot_general(a, b, (((ca,), (cb,)), ((), ())), preferred_element_type=F32)


def normalize(y):
    r = lax.rsqrt(jnp.sum(y * y, axis=-1, keepdims=True) + EPS)
    return y * r, r


def backnorm(dz, z, r):
    return r * (dz - z * jnp.sum(z * dz, axis=-1, keepdims=True))


def row_order():
    me = lax.axis_index(AXIS)
    core = me & 1
    pos = lax.broadcasted_iota(jnp.int32, (HALF, 1), 0)
    ninth = (pos * 7282) >> 16
    row = pos - 9 * ninth
    inner, outer = (ninth >> 2) & 3, (ninth >> 4) & 3
    z = (ninth & 3) ^ ((me >> 5) & 3)
    x = jnp.where(core == 0, inner, outer) ^ ((me >> 3) & 3)
    y = jnp.where(core == 0, outer, inner) ^ ((me >> 1) & 3)
    src = (((z * 4 + x) * 4 + y) * 2 + core) * 9 + row
    feature = lax.broadcasted_iota(jnp.int32, (HALF, WIDTH), 1)
    return jnp.where(feature == src, 1.0, 0.0).astype(BF)


def partners(masks_ref, mine_ref, theirs_ref, dcore):
    core = lax.axis_index(AXIS) & 1
    by_text, by_image, _ = plan(masks_ref[0], masks_ref[1])
    found = []
    for fetcher, mask in ((1, by_image), (0, by_text)):
        at = pl.multiple_of(((mask & 1) ^ core ^ dcore ^ fetcher) * ROWS, ROWS)
        rows = pl.ds(at, ROWS)
        found.append(jnp.where(core == fetcher, mine_ref[rows, :], theirs_ref[rows, :]))
    return found


def own_kernel(img_ref, txt_ref, ihead_ref, yi_ref, dimg_ref, dtxt_ref):
    yi_ref[...] = dot(img_ref[...], ihead_ref[...])
    order = row_order()
    dimg_ref[...] = dot(order, img_ref[...], 1, 1).astype(BF)
    dtxt_ref[...] = dot(order, txt_ref[...], 1, 1).astype(BF)


def local_kernel(yi_ref, txt_ref, mine_ref, theirs_ref, ihead_ref, thead_ref,
                 ls_ref, lb_ref, masks_ref, dy_ref):
    img, txt = partners(masks_ref, mine_ref, theirs_ref, 0)
    zi, ri = normalize(jnp.concatenate([yi_ref[...], dot(img, ihead_ref[...])], axis=0))
    zt, rt = normalize(dot(jnp.concatenate([txt_ref[...], txt], axis=0), thead_ref[...]))
    zib = zi.astype(BF)
    ztb = zt.astype(BF)
    scale = jnp.exp(jnp.full((1, 1), ls_ref[0], F32))
    logits = scale * dot(zib, ztb, 1, 1) + lb_ref[0]
    row = lax.broadcasted_iota(jnp.int32, logits.shape, 0)
    col = lax.broadcasted_iota(jnp.int32, logits.shape, 1)
    pos = jnp.where((row == col) & (row < ROWS), 1.0, 0.0)
    diff = 1.0 / (1.0 + jnp.exp(-logits)) - pos
    by_text, by_image, both = plan(masks_ref[0], masks_ref[1])
    apart = jnp.where(row >= ROWS, by_image, 0) ^ jnp.where(col >= ROWS, by_text, 0)
    g = jnp.where(apart == both, 0.0, diff / 16.0)
    dy_ref[:2 * ROWS, :] = backnorm(scale * dot(g.astype(BF), ztb), zi, ri).astype(BF)
    dy_ref[2 * ROWS:, :] = backnorm(scale * dot(g.T.astype(BF), zib), zt, rt).astype(BF)


def deal_kernel(img2_ref, txt2_ref, mine_ref, theirs_ref, masks_ref, dimg_ref, dtxt_ref):
    order = row_order()
    img, txt = partners(masks_ref, mine_ref, theirs_ref, 0)
    far_img, far_txt = partners(masks_ref, mine_ref, theirs_ref, 1)
    dimg_ref[...] = dot(order, jnp.concatenate([img, img2_ref[...], far_img], axis=0), 1, 1).astype(BF)
    dtxt_ref[...] = dot(order, jnp.concatenate([txt, txt2_ref[...], far_txt], axis=0), 1, 1).astype(BF)


def gradient_kernel(distances, dimg_ref, dtxt_ref, dimg2_ref, dtxt2_ref, dy_ref, dy2_ref, *outs):
    img2 = jnp.concatenate([dy_ref[ROWS:2 * ROWS, :], dy2_ref[:2 * ROWS, :]], axis=0)
    txt2 = jnp.concatenate([dy_ref[3 * ROWS:, :], dy2_ref[2 * ROWS:, :]], axis=0)
    for d, ref in zip(distances, outs):
        rows = slice(d * BLOCK, (d + 1) * BLOCK)
        img = dot(dimg_ref[rows, :], dy_ref[:ROWS, :]) + dot(dimg2_ref[rows, :], img2)
        txt = dot(dtxt_ref[rows, :], dy_ref[2 * ROWS:3 * ROWS, :]) + dot(dtxt2_ref[rows, :], txt2)
        ref[:, :WIDTH] = img.astype(ref.dtype)
        ref[:, WIDTH:] = txt.astype(ref.dtype)


def call(kernel, outs, args, scalars, flops, scalar_outs=0, grant=28, placed=pltpu.VMEM, scratch=()):
    bytes_of = lambda xs: sum(x.size * x.dtype.itemsize for x in xs)
    vmem = pl.BlockSpec(memory_space=pltpu.VMEM)
    smem = pl.BlockSpec(memory_space=pltpu.SMEM)
    return pl.pallas_call(
        kernel,
        out_shape=outs,
        in_specs=[pl.BlockSpec(memory_space=placed)] * (len(args) - scalars) + [smem] * scalars,
        out_specs=[vmem] * (len(outs) - scalar_outs) + [smem] * scalar_outs,
        scratch_shapes=scratch,
        compiler_params=pltpu.CompilerParams(vmem_limit_bytes=grant * 2**20),
        cost_estimate=pl.CostEstimate(
            flops=flops, transcendentals=0, bytes_accessed=bytes_of(args) + bytes_of(outs)),
    )(*args)


def shape(rows, cols, kind):
    return jax.ShapeDtypeStruct((rows, cols), kind)


def spread(own, sends, flips):
    got = [None] * len(sends)
    for i in (1, 0, 2):
        got[i] = swap(sends[i], *flips[i])
    got = lax.optimization_barrier(got)
    return own + got[0].astype(F32) + got[1].astype(F32) + got[2].astype(F32)


def shards(img_feat, txt_feat, img_head, txt_head, log_scale, logit_bias, masks):
    sibling = code(core=1)
    img2, txt2 = swap(img_feat, sibling), swap(txt_feat, sibling)
    mine = exchange(img_feat, txt_feat, img2, txt2, masks)
    img, txt, img2, txt2, mine = lax.optimization_barrier((img_feat, txt_feat, img2, txt2, mine))
    theirs = swap(mine, sibling)
    yi, dimg, dtxt = call(
        own_kernel, [shape(ROWS, WIDTH, F32)] + [shape(HALF, ROWS, BF)] * 2, [img, txt, img_head], 0, 10**9)
    dy, = call(
        local_kernel, [shape(4 * ROWS, WIDTH, BF)],
        [yi, txt, mine, theirs, img_head, txt_head, log_scale, logit_bias, masks], 3, 2 * 10**9)
    dy2 = swap(dy, sibling)
    dimg2, dtxt2 = call(
        deal_kernel, [shape(HALF, 3 * ROWS, BF)] * 2,
        [img2, txt2, mine, theirs, masks], 1, 2 * 10**9)

    def blocks(distances, kind):
        return call(
            functools.partial(gradient_kernel, distances), [shape(BLOCK, 2 * WIDTH, kind)] * len(distances),
            [dimg, dtxt, dimg2, dtxt2, dy, dy2], 0, len(distances) * 4 * 10**8)

    second, = blocks((2,), BF)
    first, third = blocks((1, 3), BF)
    kept, = blocks((0,), F32)
    total = spread(kept, (first, second, third), [(code(y=d), code(x=d)) for d in (1, 2, 3)])
    rows = [total[d * GROUP:(d + 1) * GROUP] for d in range(4)]
    total = spread(rows[0], [r.astype(BF) for r in rows[1:]], [(code(x=d), code(y=d)) for d in (1, 2, 3)])

    high = lax.axis_index(AXIS) >= code(z=4)
    img, txt = total[:, :WIDTH], total[:, WIDTH:]
    near, far = jnp.where(high, txt, img), jnp.where(high, img, txt)
    far = jnp.concatenate([far[i * 9:i * 9 + 9] for i in (3, 2, 1, 0)], axis=0)
    total = near + swap(far.astype(BF), code(z=7)).astype(F32)
    rows = [total[d * 9:d * 9 + 9] for d in range(4)]
    total = spread(rows[0], [r.astype(BF) for r in rows[1:]], [(code(z=d),) for d in (1, 2, 3)])
    return total.reshape(81, 128)


def solution(mesh):
    return jax.shard_map(
        shards,
        mesh=mesh,
        in_specs=(P("dp", None), P("dp", None), P(), P(), P(), P(), P()),
        out_specs=P("dp", None),
        check_vma=False,
    )
```

```python
import functools

import jax
import jax.numpy as jnp
from jax import lax
from jax.experimental import pallas as pl
from jax.experimental.pallas import tpu as pltpu
from jax.sharding import PartitionSpec as P

EPS = 1e-06
AXIS = "dp"
NZ, NX, NY, NCORE = 8, 4, 4, 2
BF = jnp.bfloat16
F32 = jnp.float32
ROWS, WIDTH = 160, 1152
HALF = WIDTH // 2
GROUP = 36
BLOCK = 4 * GROUP


def swap(x, flip, odd_flip=None):
    flips = (flip, flip if odd_flip is None else odd_flip)
    return lax.ppermute(x, AXIS, [(i, i ^ flips[i % NCORE]) for i in range(NZ * NX * NY * NCORE)])


def code(z=0, x=0, y=0, core=0):
    return ((z * NX + x) * NY + y) * NCORE + core


def plan(first, second):
    both = first ^ second
    low, high = jnp.minimum(first, second), jnp.maximum(first, second)
    return jnp.maximum(high, both), jnp.minimum(low, both), both


def start_kernel(img_hbm, txt_hbm, masks_hbm, own_ref, first_ref, second_ref, masks_ref, arrived):
    even = lax.axis_index(AXIS) & 1 == 0
    load = pltpu.make_async_copy(masks_hbm, masks_ref, arrived.at[0])
    load.start()

    @pl.when(even)
    def _():
        pltpu.make_async_copy(txt_hbm, own_ref, arrived.at[1]).start()

    @pl.when(jnp.logical_not(even))
    def _():
        pltpu.make_async_copy(img_hbm, own_ref, arrived.at[1]).start()

    load.wait()
    by_text, by_image, _ = plan(masks_ref[0], masks_ref[1])
    mask = jnp.where(even, by_text, by_image)
    along_z = mask >> 5
    along_xy = NZ + ((mask >> 1) & 15)
    first_ref[0] = jnp.where(even, along_z, along_xy)
    second_ref[0] = jnp.where(even, along_xy, along_z)
    pltpu.make_async_copy(txt_hbm, own_ref, arrived.at[1]).wait()


def exchange(img, txt, img2, txt2, masks):
    even = lax.axis_index(AXIS) & 1 == 0
    flips = [code(z=p) for p in range(NZ)] + [code(x=q // NY, y=q % NY) for q in range(NX * NY)]
    branches = [lambda a, f=f: swap(a, f) if f else a for f in flips]
    index = jax.ShapeDtypeStruct((1,), jnp.int32)
    own, first, second = call(
        start_kernel, [shape(ROWS, WIDTH, BF), index, index], [img, txt, masks], 0, 10**6, scalar_outs=2,
        grant=60, placed=pl.ANY, scratch=[pltpu.SMEM((2,), jnp.int32), pltpu.SemaphoreType.DMA((2,))])
    got = jnp.concatenate([own, jnp.where(even, txt2, img2)], axis=0)
    got = lax.switch(first[0], branches, got)
    got, second = lax.optimization_barrier((got, second))
    return lax.switch(second[0], branches, got)


def dot(a, b, ca=1, cb=0):
    return lax.dot_general(a, b, (((ca,), (cb,)), ((), ())), preferred_element_type=F32)


def normalize(y):
    r = lax.rsqrt(jnp.sum(y * y, axis=-1, keepdims=True) + EPS)
    return y * r, r


def backnorm(dz, z, r):
    return r * (dz - z * jnp.sum(z * dz, axis=-1, keepdims=True))


def row_order():
    me = lax.axis_index(AXIS)
    core = me & 1
    pos = lax.broadcasted_iota(jnp.int32, (HALF, 1), 0)
    ninth = (pos * 7282) >> 16
    row = pos - 9 * ninth
    inner, outer = (ninth >> 2) & 3, (ninth >> 4) & 3
    z = (ninth & 3) ^ ((me >> 5) & 3)
    x = jnp.where(core == 0, inner, outer) ^ ((me >> 3) & 3)
    y = jnp.where(core == 0, outer, inner) ^ ((me >> 1) & 3)
    src = (((z * 4 + x) * 4 + y) * 2 + core) * 9 + row
    feature = lax.broadcasted_iota(jnp.int32, (HALF, WIDTH), 1)
    return jnp.where(feature == src, 1.0, 0.0).astype(BF)


def partners(masks_ref, mine_ref, theirs_ref, dcore):
    core = lax.axis_index(AXIS) & 1
    by_text, by_image, _ = plan(masks_ref[0], masks_ref[1])
    found = []
    for fetcher, mask in ((1, by_image), (0, by_text)):
        at = pl.multiple_of(((mask & 1) ^ core ^ dcore ^ fetcher) * ROWS, ROWS)
        rows = pl.ds(at, ROWS)
        found.append(jnp.where(core == fetcher, mine_ref[rows, :], theirs_ref[rows, :]))
    return found


def own_kernel(img_ref, txt_ref, ihead_ref, yi_ref, dimg_ref, dtxt_ref):
    yi_ref[...] = dot(img_ref[...], ihead_ref[...])
    order = row_order()
    dimg_ref[...] = dot(order, img_ref[...], 1, 1).astype(BF)
    dtxt_ref[...] = dot(order, txt_ref[...], 1, 1).astype(BF)


def local_kernel(yi_ref, txt_ref, mine_ref, theirs_ref, ihead_ref, thead_ref,
                 ls_ref, lb_ref, masks_ref, dy_ref):
    img, txt = partners(masks_ref, mine_ref, theirs_ref, 0)
    zi, ri = normalize(jnp.concatenate([yi_ref[...], dot(img, ihead_ref[...])], axis=0))
    zt, rt = normalize(dot(jnp.concatenate([txt_ref[...], txt], axis=0), thead_ref[...]))
    zib = zi.astype(BF)
    ztb = zt.astype(BF)
    scale = jnp.exp(ls_ref[...].reshape(1, 1))
    logits = scale * dot(zib, ztb, 1, 1) + lb_ref[...].reshape(1, 1)
    row = lax.broadcasted_iota(jnp.int32, logits.shape, 0)
    col = lax.broadcasted_iota(jnp.int32, logits.shape, 1)
    pos = jnp.where((row == col) & (row < ROWS), 1.0, 0.0)
    diff = 1.0 / (1.0 + jnp.exp(-logits)) - pos
    by_text, by_image, both = plan(masks_ref[0], masks_ref[1])
    apart = jnp.where(row >= ROWS, by_image, 0) ^ jnp.where(col >= ROWS, by_text, 0)
    g = jnp.where(apart == both, 0.0, diff / 16.0)
    dy_ref[:2 * ROWS, :] = backnorm(scale * dot(g.astype(BF), ztb), zi, ri).astype(BF)
    dy_ref[2 * ROWS:, :] = backnorm(scale * dot(g.T.astype(BF), zib), zt, rt).astype(BF)


def deal_kernel(img2_ref, txt2_ref, mine_ref, theirs_ref, masks_ref, dimg_ref, dtxt_ref):
    order = row_order()
    img, txt = partners(masks_ref, mine_ref, theirs_ref, 0)
    far_img, far_txt = partners(masks_ref, mine_ref, theirs_ref, 1)
    dimg_ref[...] = dot(order, jnp.concatenate([img, img2_ref[...], far_img], axis=0), 1, 1).astype(BF)
    dtxt_ref[...] = dot(order, jnp.concatenate([txt, txt2_ref[...], far_txt], axis=0), 1, 1).astype(BF)


def gradient_kernel(distances, dimg_ref, dtxt_ref, dimg2_ref, dtxt2_ref, dy_ref, dy2_ref, *outs):
    img2 = jnp.concatenate([dy_ref[ROWS:2 * ROWS, :], dy2_ref[:2 * ROWS, :]], axis=0)
    txt2 = jnp.concatenate([dy_ref[3 * ROWS:, :], dy2_ref[2 * ROWS:, :]], axis=0)
    for d, ref in zip(distances, outs):
        rows = slice(d * BLOCK, (d + 1) * BLOCK)
        img = dot(dimg_ref[rows, :], dy_ref[:ROWS, :]) + dot(dimg2_ref[rows, :], img2)
        txt = dot(dtxt_ref[rows, :], dy_ref[2 * ROWS:3 * ROWS, :]) + dot(dtxt2_ref[rows, :], txt2)
        ref[:, :WIDTH] = img.astype(ref.dtype)
        ref[:, WIDTH:] = txt.astype(ref.dtype)


def call(kernel, outs, args, scalars, flops, scalar_outs=0, grant=28, placed=pltpu.VMEM, scratch=()):
    bytes_of = lambda xs: sum(x.size * x.dtype.itemsize for x in xs)
    vmem = pl.BlockSpec(memory_space=pltpu.VMEM)
    smem = pl.BlockSpec(memory_space=pltpu.SMEM)
    return pl.pallas_call(
        kernel,
        out_shape=outs,
        in_specs=[pl.BlockSpec(memory_space=placed)] * (len(args) - scalars) + [smem] * scalars,
        out_specs=[vmem] * (len(outs) - scalar_outs) + [smem] * scalar_outs,
        scratch_shapes=scratch,
        compiler_params=pltpu.CompilerParams(vmem_limit_bytes=grant * 2**20),
        cost_estimate=pl.CostEstimate(
            flops=flops, transcendentals=0, bytes_accessed=bytes_of(args) + bytes_of(outs)),
    )(*args)


def shape(rows, cols, kind):
    return jax.ShapeDtypeStruct((rows, cols), kind)


def spread(own, sends, flips):
    got = [None] * len(sends)
    for i in (1, 0, 2):
        got[i] = swap(sends[i], *flips[i])
    got = lax.optimization_barrier(got)
    return own + got[0].astype(F32) + got[1].astype(F32) + got[2].astype(F32)


def shards(img_feat, txt_feat, img_head, txt_head, log_scale, logit_bias, masks):
    sibling = code(core=1)
    img2, txt2 = swap(img_feat, sibling), swap(txt_feat, sibling)
    mine = exchange(img_feat, txt_feat, img2, txt2, masks)
    img, txt, img2, txt2, mine = lax.optimization_barrier((img_feat, txt_feat, img2, txt2, mine))
    theirs = swap(mine, sibling)
    yi, dimg, dtxt = call(
        own_kernel, [shape(ROWS, WIDTH, F32)] + [shape(HALF, ROWS, BF)] * 2, [img, txt, img_head], 0, 10**9)
    dy, = call(
        local_kernel, [shape(4 * ROWS, WIDTH, BF)],
        [yi, txt, mine, theirs, img_head, txt_head, log_scale, logit_bias, masks],
        1, 2 * 10**9)
    dy2 = swap(dy, sibling)
    dimg2, dtxt2 = call(
        deal_kernel, [shape(HALF, 3 * ROWS, BF)] * 2,
        [img2, txt2, mine, theirs, masks], 1, 2 * 10**9)

    def blocks(distances, kind):
        return call(
            functools.partial(gradient_kernel, distances), [shape(BLOCK, 2 * WIDTH, kind)] * len(distances),
            [dimg, dtxt, dimg2, dtxt2, dy, dy2], 0, len(distances) * 4 * 10**8)

    second, = blocks((2,), BF)
    first, third = blocks((1, 3), BF)
    kept, = blocks((0,), F32)
    total = spread(kept, (first, second, third), [(code(y=d), code(x=d)) for d in (1, 2, 3)])
    rows = [total[d * GROUP:(d + 1) * GROUP] for d in range(4)]
    total = spread(rows[0], [r.astype(BF) for r in rows[1:]], [(code(x=d), code(y=d)) for d in (1, 2, 3)])

    high = lax.axis_index(AXIS) >= code(z=4)
    img, txt = total[:, :WIDTH], total[:, WIDTH:]
    near, far = jnp.where(high, txt, img), jnp.where(high, img, txt)
    far = jnp.concatenate([far[i * 9:i * 9 + 9] for i in (3, 2, 1, 0)], axis=0)
    total = near + swap(far.astype(BF), code(z=7)).astype(F32)
    rows = [total[d * 9:d * 9 + 9] for d in range(4)]
    total = spread(rows[0], [r.astype(BF) for r in rows[1:]], [(code(z=d),) for d in (1, 2, 3)])
    return total.reshape(81, 128)


def solution(mesh):
    return jax.shard_map(
        shards,
        mesh=mesh,
        in_specs=(P("dp", None), P("dp", None), P(), P(), P(), P(), P()),
        out_specs=P("dp", None),
        check_vma=False,
    )
```

```python
import functools

import jax
import jax.numpy as jnp
from jax import lax
from jax.experimental import pallas as pl
from jax.experimental.pallas import tpu as pltpu
from jax.sharding import PartitionSpec as P

EPS = 1e-06
AXIS = "dp"
NZ, NX, NY, NCORE = 8, 4, 4, 2
BF = jnp.bfloat16
F32 = jnp.float32
ROWS, WIDTH = 160, 1152
HALF = WIDTH // 2
GROUP = 36
BLOCK = 4 * GROUP


def swap(x, flip, odd_flip=None):
    flips = (flip, flip if odd_flip is None else odd_flip)
    return lax.ppermute(x, AXIS, [(i, i ^ flips[i % NCORE]) for i in range(NZ * NX * NY * NCORE)])


def code(z=0, x=0, y=0, core=0):
    return ((z * NX + x) * NY + y) * NCORE + core


def plan(first, second):
    both = first ^ second
    low, high = jnp.minimum(first, second), jnp.maximum(first, second)
    return jnp.maximum(high, both), jnp.minimum(low, both), both


def start_kernel(img_hbm, txt_hbm, masks_hbm, own_ref, first_ref, second_ref, masks_ref, arrived):
    even = lax.axis_index(AXIS) & 1 == 0
    load = pltpu.make_async_copy(masks_hbm, masks_ref, arrived.at[0])
    load.start()

    @pl.when(even)
    def _():
        pltpu.make_async_copy(txt_hbm, own_ref, arrived.at[1]).start()

    @pl.when(jnp.logical_not(even))
    def _():
        pltpu.make_async_copy(img_hbm, own_ref, arrived.at[1]).start()

    load.wait()
    by_text, by_image, _ = plan(masks_ref[0], masks_ref[1])
    mask = jnp.where(even, by_text, by_image)
    along_z = mask >> 5
    along_xy = NZ + ((mask >> 1) & 15)
    first_ref[0] = jnp.where(even, along_z, along_xy)
    second_ref[0] = jnp.where(even, along_xy, along_z)
    pltpu.make_async_copy(txt_hbm, own_ref, arrived.at[1]).wait()


def exchange(img, txt, img2, txt2, masks):
    even = lax.axis_index(AXIS) & 1 == 0
    flips = [code(z=p) for p in range(NZ)] + [code(x=q // NY, y=q % NY) for q in range(NX * NY)]
    branches = [lambda a, f=f: swap(a, f) if f else a for f in flips]
    index = jax.ShapeDtypeStruct((1,), jnp.int32)
    own, first, second = call(
        start_kernel, [shape(ROWS, WIDTH, BF), index, index], [img, txt, masks], 0, 10**6, scalar_outs=2,
        grant=60, placed=pl.ANY, scratch=[pltpu.SMEM((2,), jnp.int32), pltpu.SemaphoreType.DMA((2,))])
    got = jnp.concatenate([own, jnp.where(even, txt2, img2)], axis=0)
    got = lax.switch(first[0], branches, got)
    got, second = lax.optimization_barrier((got, second))
    return lax.switch(second[0], branches, got)


def dot(a, b, ca=1, cb=0):
    return lax.dot_general(a, b, (((ca,), (cb,)), ((), ())), preferred_element_type=F32)


def normalize(y):
    r = lax.rsqrt(jnp.sum(y * y, axis=-1, keepdims=True) + EPS)
    return y * r, r


def backnorm(dz, z, r):
    return r * (dz - z * jnp.sum(z * dz, axis=-1, keepdims=True))


def row_order():
    me = lax.axis_index(AXIS)
    core = me & 1
    pos = lax.broadcasted_iota(jnp.int32, (HALF, 1), 0)
    ninth = (pos * 7282) >> 16
    row = pos - 9 * ninth
    inner, outer = (ninth >> 2) & 3, (ninth >> 4) & 3
    z = (ninth & 3) ^ ((me >> 5) & 3)
    x = jnp.where(core == 0, inner, outer) ^ ((me >> 3) & 3)
    y = jnp.where(core == 0, outer, inner) ^ ((me >> 1) & 3)
    src = (((z * 4 + x) * 4 + y) * 2 + core) * 9 + row
    feature = lax.broadcasted_iota(jnp.int32, (HALF, WIDTH), 1)
    return jnp.where(feature == src, 1.0, 0.0).astype(BF)


def partners(masks_ref, mine_ref, theirs_ref, dcore):
    core = lax.axis_index(AXIS) & 1
    by_text, by_image, _ = plan(masks_ref[0], masks_ref[1])
    found = []
    for fetcher, mask in ((1, by_image), (0, by_text)):
        at = pl.multiple_of(((mask & 1) ^ core ^ dcore ^ fetcher) * ROWS, ROWS)
        rows = pl.ds(at, ROWS)
        found.append(jnp.where(core == fetcher, mine_ref[rows, :], theirs_ref[rows, :]))
    return found


def own_kernel(img_ref, txt_ref, ihead_ref, yi_ref, dimg_ref, dtxt_ref):
    yi_ref[...] = dot(img_ref[...], ihead_ref[...])
    order = row_order()
    dimg_ref[...] = dot(order, img_ref[...], 1, 1).astype(BF)
    dtxt_ref[...] = dot(order, txt_ref[...], 1, 1).astype(BF)


def local_kernel(yi_ref, txt_ref, mine_ref, theirs_ref, ihead_ref, thead_ref,
                 ls_ref, lb_ref, masks_ref, dy_ref):
    img, txt = partners(masks_ref, mine_ref, theirs_ref, 0)
    zi, ri = normalize(jnp.concatenate([yi_ref[...], dot(img, ihead_ref[...])], axis=0))
    zt, rt = normalize(dot(jnp.concatenate([txt_ref[...], txt], axis=0), thead_ref[...]))
    zib = zi.astype(BF)
    ztb = zt.astype(BF)
    scale = jnp.exp(ls_ref[...].reshape(1, 1))
    logits = scale * dot(zib, ztb, 1, 1) + lb_ref[...].reshape(1, 1)
    row = lax.broadcasted_iota(jnp.int32, logits.shape, 0)
    col = lax.broadcasted_iota(jnp.int32, logits.shape, 1)
    pos = jnp.where((row == col) & (row < ROWS), 1.0, 0.0)
    diff = 1.0 / (1.0 + jnp.exp(-logits)) - pos
    by_text, by_image, both = plan(masks_ref[0], masks_ref[1])
    apart = jnp.where(row >= ROWS, by_image, 0) ^ jnp.where(col >= ROWS, by_text, 0)
    g = jnp.where(apart == both, 0.0, diff / 16.0)
    dy_ref[:2 * ROWS, :] = backnorm(scale * dot(g.astype(BF), ztb), zi, ri).astype(BF)
    dy_ref[2 * ROWS:, :] = backnorm(scale * dot(g.T.astype(BF), zib), zt, rt).astype(BF)


def deal_kernel(img2_ref, txt2_ref, mine_ref, theirs_ref, masks_ref, dimg_ref, dtxt_ref):
    order = row_order()
    img, txt = partners(masks_ref, mine_ref, theirs_ref, 0)
    far_img, far_txt = partners(masks_ref, mine_ref, theirs_ref, 1)
    dimg_ref[...] = dot(order, jnp.concatenate([img, img2_ref[...], far_img], axis=0), 1, 1).astype(BF)
    dtxt_ref[...] = dot(order, jnp.concatenate([txt, txt2_ref[...], far_txt], axis=0), 1, 1).astype(BF)


def gradient_kernel(distances, dimg_ref, dtxt_ref, dimg2_ref, dtxt2_ref, dy_ref, dy2_ref, *outs):
    img2 = jnp.concatenate([dy_ref[ROWS:2 * ROWS, :], dy2_ref[:2 * ROWS, :]], axis=0)
    txt2 = jnp.concatenate([dy_ref[3 * ROWS:, :], dy2_ref[2 * ROWS:, :]], axis=0)
    for d, ref in zip(distances, outs):
        rows = slice(d * BLOCK, (d + 1) * BLOCK)
        img = dot(dimg_ref[rows, :], dy_ref[:ROWS, :]) + dot(dimg2_ref[rows, :], img2)
        txt = dot(dtxt_ref[rows, :], dy_ref[2 * ROWS:3 * ROWS, :]) + dot(dtxt2_ref[rows, :], txt2)
        ref[:, :WIDTH] = img.astype(ref.dtype)
        ref[:, WIDTH:] = txt.astype(ref.dtype)


def call(kernel, outs, args, scalars, flops, scalar_outs=0, grant=28, placed=pltpu.VMEM, scratch=()):
    bytes_of = lambda xs: sum(x.size * x.dtype.itemsize for x in xs)
    vmem = pl.BlockSpec(memory_space=pltpu.VMEM)
    smem = pl.BlockSpec(memory_space=pltpu.SMEM)
    return pl.pallas_call(
        kernel,
        out_shape=outs,
        in_specs=[pl.BlockSpec(memory_space=placed)] * (len(args) - scalars) + [smem] * scalars,
        out_specs=[vmem] * (len(outs) - scalar_outs) + [smem] * scalar_outs,
        scratch_shapes=scratch,
        compiler_params=pltpu.CompilerParams(vmem_limit_bytes=grant * 2**20),
        cost_estimate=pl.CostEstimate(
            flops=flops, transcendentals=0, bytes_accessed=bytes_of(args) + bytes_of(outs)),
    )(*args)


def shape(rows, cols, kind):
    return jax.ShapeDtypeStruct((rows, cols), kind)


def spread(own, sends, flips):
    got = [None] * len(sends)
    for i in (1, 0, 2):
        got[i] = swap(sends[i], *flips[i])
    got = lax.optimization_barrier(got)
    return own + got[0].astype(F32) + got[1].astype(F32) + got[2].astype(F32)


def shards(img_feat, txt_feat, img_head, txt_head, log_scale, logit_bias, masks):
    sibling = code(core=1)
    img2, txt2 = swap(img_feat, sibling), swap(txt_feat, sibling)
    mine = exchange(img_feat, txt_feat, img2, txt2, masks)
    img, txt, img2, txt2, mine = lax.optimization_barrier((img_feat, txt_feat, img2, txt2, mine))
    theirs = swap(mine, sibling)
    yi, dimg, dtxt = call(
        own_kernel, [shape(ROWS, WIDTH, F32)] + [shape(HALF, ROWS, BF)] * 2, [img, txt, img_head], 0, 10**9)
    dy, = call(
        local_kernel, [shape(4 * ROWS, WIDTH, BF)],
        [yi, txt, mine, theirs, img_head, txt_head, log_scale, logit_bias, masks],
        1, 2 * 10**9)
    dy2 = swap(dy, sibling)
    dimg2, dtxt2 = call(
        deal_kernel, [shape(HALF, 3 * ROWS, BF)] * 2,
        [img2, txt2, mine, theirs, masks], 1, 2 * 10**9)

    def blocks(distances, kind):
        return call(
            functools.partial(gradient_kernel, distances), [shape(BLOCK, 2 * WIDTH, kind)] * len(distances),
            [dimg, dtxt, dimg2, dtxt2, dy, dy2], 0, len(distances) * 4 * 10**8)

    second, = blocks((2,), BF)
    second, dy2 = lax.optimization_barrier((second, dy2))
    first, = blocks((1,), BF)
    first, dy2 = lax.optimization_barrier((first, dy2))
    third, = blocks((3,), BF)
    kept, = blocks((0,), F32)
    total = spread(kept, (first, second, third), [(code(y=d), code(x=d)) for d in (1, 2, 3)])
    rows = [total[d * GROUP:(d + 1) * GROUP] for d in range(4)]
    total = spread(rows[0], [r.astype(BF) for r in rows[1:]], [(code(x=d), code(y=d)) for d in (1, 2, 3)])

    high = lax.axis_index(AXIS) >= code(z=4)
    img, txt = total[:, :WIDTH], total[:, WIDTH:]
    near, far = jnp.where(high, txt, img), jnp.where(high, img, txt)
    far = jnp.concatenate([far[i * 9:i * 9 + 9] for i in (3, 2, 1, 0)], axis=0)
    total = near + swap(far.astype(BF), code(z=7)).astype(F32)
    rows = [total[d * 9:d * 9 + 9] for d in range(4)]
    total = spread(rows[0], [r.astype(BF) for r in rows[1:]], [(code(z=d),) for d in (1, 2, 3)])
    return total.reshape(81, 128)


def solution(mesh):
    return jax.shard_map(
        shards,
        mesh=mesh,
        in_specs=(P("dp", None), P("dp", None), P(), P(), P(), P(), P()),
        out_specs=P("dp", None),
        check_vma=False,
    )
```
